32 devices in a mesh: gx: 8 (over y, x, core), gy: 4 (over z).
Axes of the slice: x: 2, y: 2, z: 4, core: 2. Of those that a mesh axis runs over, the one named last changes fastest.
Arguments:
- diffusivity: float32 [256, 512], P('gx', 'gy'), may hold values from 0.25 to 1
- base_humidity: float32 [256, 512], P('gx', 'gy'), may hold values from -4 to 4
- coupling: float32 [256, 512], P('gx', 'gy'), may hold values from 0.1 to 0.4
- basis_rows: float32 [256, 64], P('gx'), may hold values from -0.45 to 0.45
- basis_cols: float32 [512, 32], P('gy'), may hold values from -0.45 to 0.45
- directions: float32 [16, 64, 32], replicated, may hold values from -5 to 5
- send_cell: int32 [8, 4, 8, 8], P('gx', 'gy'), may hold values from 0 to 4095
- send_weight: float32 [8, 4, 8, 8], P('gx', 'gy'), may hold values from 0.1 to 1
- send_count: int32 [8, 4, 8], P('gx', 'gy'), may hold values from 1 to 8, as said below
- owner_gauge: int32 [8, 4, 8, 8], P('gx', 'gy'), may hold values from 0 to 39
- noise_precision: float32 [8, 4, 40], P('gx', 'gy'), may hold values from 1 to 16
Outputs:
- readings: float32 [8, 4, 16, 40], P('gx', 'gy')
- hess_action: float32 [16, 64, 32], replicated
The draws below stay inside these ranges and needn't reach their ends.
Inputs may be any that keep to these rules, and one draw needn't show every extreme that they name: `send_count`: entries from one device to one owner; in every draw, in each row of the gy axis one owner receives exactly 8 from every device. `send_cell`: A local cell index of the sending device. `owner_gauge`: A gauge of the owner.
All inputs are finite; a program needn't handle non-finite values.
Results may differ from the reference program's by a relative error of at most 0.00011.
Values sent between devices are 32-bit elements; how exact they have to be, the bound alone decides.
A program may use at most 64 MiB of HBM per device.

```python
import math
import jax
import jax.numpy as jnp
from jax import lax

CX = 32
CY = 128
DIRS = 16
MODES_X = 64
MODES_Y = 32
STEPS = 6
SLOT = 8
GAUGES = 40
NX = 256
NY = 512
N_GX = 8
N_GY = 4


def draw_send_count(key, part):
    first_key, second_key = jax.random.split(jax.random.fold_in(key, 17))
    counts = jax.random.randint(first_key, (N_GX, N_GY, N_GX), 1, SLOT + 1)
    offset = jax.random.randint(second_key, (), 0, N_GX)
    full_owner = (offset + 3 * jnp.arange(N_GY, dtype=jnp.int32)) % N_GX
    owner_ids = jnp.arange(N_GX, dtype=jnp.int32)[None, None, :]
    is_full = owner_ids == full_owner[None, :, None]
    return jnp.where(is_full, SLOT, counts).astype(jnp.int32)


def set_ends(entries, own_key, low, top_value):
    shape = entries.shape
    spot = [jax.random.randint(jax.random.fold_in(own_key, axis), (), 0, shape[axis]) for axis in range(len(shape))]
    entries = entries.at[tuple(spot)].set(low)
    longest = shape.index(max(shape))
    spot[longest] = (spot[longest] + 1) % shape[longest]
    return entries.at[tuple(spot)].set(top_value)


def shard_levels(stream_key, shape, cuts, smallest, largest):
    level, own = 1.0, jax.random.fold_in(stream_key, 6)
    for position, shards_of in cuts:
        heights = jnp.exp(jax.random.uniform(jax.random.fold_in(own, position), (shards_of,), jnp.float32, smallest / len(cuts), largest / len(cuts)))
        level = level * jnp.repeat(heights, shape[position] // shards_of).reshape([-1 if axis == position else 1 for axis in range(len(shape))])
    return level


def centred(own_key, dims, deviation, bound, shards=(), kind=jnp.bfloat16):
    array = jax.random.normal(own_key, dims, jnp.float32) * deviation
    if len(shards) > 0:
        array = shard_levels(own_key, dims, shards, -0.22, 0.18) * array
    return jnp.clip(array, min=-bound, max=bound).astype(kind)


def setup_inputs(seed: int = 0) -> dict:
    keys = jax.random.split(jax.random.key(seed), 12)
    return {
        "diffusivity": jnp.clip(jnp.exp(math.log(1.0) - 1.3862944 * jax.random.uniform(keys[0], (NX, NY), jnp.float32) ** shard_levels(keys[0], (NX, NY), ((0, 8), (1, 4)), -0.2, 0.2)), 0.25, 1.0),
        "base_humidity": centred(keys[1], (NX, NY), 1.0, 4.0, ((0, 8), (1, 4)), jnp.float32),
        "coupling": jnp.clip(jnp.exp(math.log(0.4) - 1.3862944 * jax.random.uniform(keys[2], (NX, NY), jnp.float32) ** shard_levels(keys[2], (NX, NY), ((0, 8), (1, 4)), -0.2, 0.2)), 0.1, 0.4),
        "basis_rows": centred(keys[3], (NX, MODES_X), 0.075, 0.45, ((0, 8),), jnp.float32),
        "basis_cols": centred(keys[4], (NY, MODES_Y), 0.075, 0.45, ((0, 4),), jnp.float32),
        "directions": centred(keys[5], (DIRS, MODES_X, MODES_Y), 1.0, 5.0, (), jnp.float32),
        "send_cell": set_ends(jax.random.randint(keys[6], (N_GX, N_GY, N_GX, SLOT), 0, CX * CY), jax.random.fold_in(keys[6], 1), 0, (CX * CY) - 1).astype(jnp.int32),
        "send_weight": jnp.clip(0.1 + 0.9 * jax.random.uniform(keys[7], (N_GX, N_GY, N_GX, SLOT), jnp.float32) ** shard_levels(keys[7], (N_GX, N_GY, N_GX, SLOT), ((0, 8), (1, 4)), -0.2, 0.2), 0.1, 1.0),
        "send_count": draw_send_count(jax.random.fold_in(keys[11], 71), 0),
        "owner_gauge": set_ends(jax.random.randint(keys[9], (N_GX, N_GY, N_GX, SLOT), 0, GAUGES), jax.random.fold_in(keys[9], 1), 0, GAUGES - 1).astype(jnp.int32),
        "noise_precision": jnp.clip(jnp.exp(math.log(16.0) - 2.7725887 * jax.random.uniform(keys[10], (N_GX, N_GY, GAUGES), jnp.float32) ** shard_levels(keys[10], (N_GX, N_GY, GAUGES), ((0, 8), (1, 4)), -0.2, 0.2)), 1.0, 16.0),
    }


step_ratio = 0.2
exact = lax.Precision.HIGHEST


def bordered(field):
    return jnp.pad(field, [(0, 0)] * (field.ndim - 2) + [(1, 1), (1, 1)])


def spread(field):
    middle = field[..., 1:-1, 1:-1]
    return middle, (field[..., :-2, 1:-1], field[..., 2:, 1:-1], field[..., 1:-1, :-2], field[..., 1:-1, 2:])


def update(temper, humid, diff_pad, coupling, orient):
    temp_mid, temp_near = spread(bordered(temper))
    hum_mid, hum_near = spread(bordered(humid))
    diff_mid, diff_near = spread(diff_pad)
    lap_temp = sum(n - temp_mid for n in temp_near)
    lap_hum = sum(0.5 * (diff_mid + k) * (n - hum_mid) for k, n in zip(diff_near, hum_near))
    new_temp = temp_mid + step_ratio * lap_temp + orient * coupling * hum_mid
    new_hum = hum_mid + step_ratio * lap_hum - orient * coupling * temp_mid
    return new_temp, new_hum


def reference(diffusivity, base_humidity, coupling, basis_rows, basis_cols, directions, send_cell, send_weight, send_count, owner_gauge, noise_precision):
    sender = jnp.arange(N_GX, dtype=jnp.int32)[:, None, None, None]
    column_dev = jnp.arange(N_GY, dtype=jnp.int32)[None, :, None, None]
    owner = jnp.arange(N_GX, dtype=jnp.int32)[None, None, :, None]
    slot_idx = jnp.arange(SLOT, dtype=jnp.int32)[None, None, None, :]
    row_global = sender * CX + send_cell // CY
    col_global = column_dev * CY + send_cell % CY
    cell_index = (row_global * NY + col_global).reshape(-1).astype(jnp.int32)
    live_mask = (slot_idx < send_count[..., None]).astype(jnp.float32)
    factor = (send_weight * live_mask).reshape(-1)
    gauge_sent = jnp.transpose(owner_gauge, (2, 1, 0, 3))
    gauge_index = ((owner * N_GY + column_dev) * GAUGES + gauge_sent).reshape(-1).astype(jnp.int32)
    diff_pad = bordered(diffusivity)
    hum_pad = bordered(base_humidity)
    hum_mid, hum_near = spread(hum_pad)
    weights_flat = noise_precision.reshape(-1)

    def one_direction(vector):
        perturb = jnp.dot(jnp.dot(basis_rows, vector, precision=exact), basis_cols.T, precision=exact)
        param_mid, param_near = spread(bordered(diffusivity * perturb))
        source = sum(0.5 * (param_mid + p) * (h - hum_mid) for p, h in zip(param_near, hum_near))
        temper = jnp.zeros_like(source)
        humid = step_ratio * source
        for i in range(STEPS - 1):
            temper, humid = update(temper, humid, diff_pad, coupling, 1.0)
            humid = humid + step_ratio * source
        picked = humid.reshape(-1)[cell_index] * factor
        gauge_read = jax.ops.segment_sum(picked, gauge_index, num_segments=N_GX * N_GY * GAUGES)
        weighted = weights_flat * gauge_read
        returned = weighted[gauge_index] * factor
        adjoint_load = jax.ops.segment_sum(returned, cell_index, num_segments=NX * NY).reshape(NX, NY)
        adj_temp = jnp.zeros_like(adjoint_load)
        adj_hum = adjoint_load
        summed = adjoint_load
        for i in range(STEPS - 1):
            adj_temp, adj_hum = update(adj_temp, adj_hum, diff_pad, coupling, -1.0)
            summed = summed + adj_hum
        lam_field = step_ratio * summed
        lam_mid, lam_near = spread(bordered(lam_field))
        gradient = diffusivity * sum(0.5 * (h - hum_mid) * (lam_mid - l) for h, l in zip(hum_near, lam_near))
        projected = jnp.dot(jnp.dot(basis_rows.T, gradient, precision=exact), basis_cols, precision=exact)
        return gauge_read, vector + projected

    gauge_all, hess_action = lax.map(one_direction, directions)
    readings = jnp.transpose(gauge_all.reshape(DIRS, N_GX, N_GY, GAUGES), (1, 2, 0, 3))
    return readings, hess_action
```

```python
import functools

import jax
import jax.numpy as jnp
from jax import lax
from jax.experimental import pallas as pl
from jax.experimental.pallas import tpu as pltpu
from jax.sharding import PartitionSpec as P

STEPS = 6
step_ratio = 0.2
exact = lax.Precision.HIGHEST
f32 = jnp.float32
bf16 = jnp.bfloat16
PAD = 8
NN = (((1,), (0,)), ((), ()))
NT = (((1,), (1,)), ((), ()))


def iota(shape, dim):
    return lax.broadcasted_iota(jnp.int32, shape, dim)


def dot(a, b, dims=NN):
    return lax.dot_general(a, b, dims, precision=exact, preferred_element_type=f32)


def pick_dot(values, hot, dims=NN):
    hot = hot.astype(bf16)
    total = None
    for _ in range(3):
        part = values.astype(bf16)
        values = values - part.astype(f32)
        term = lax.dot_general(part, hot, dims, preferred_element_type=f32)
        total = term if total is None else total + term
    return total


def around(v):
    rows, cols = v.shape
    return (
        pltpu.roll(v, 1, 0),
        pltpu.roll(v, rows - 1, 0),
        pltpu.roll(v, 1, 1),
        pltpu.roll(v, cols - 1, 1),
    )


def turned(v):
    rows, cols = v.shape
    if cols % 128:
        v = jnp.concatenate([v, jnp.zeros((rows, 128 - cols % 128), f32)], axis=1)
    if rows % 128:
        v = jnp.concatenate([v, jnp.zeros((128 - rows % 128, v.shape[1]), f32)], axis=0)
    return v.T


def column(row):
    m = row.shape[1]
    same = iota((m, m), 0) == iota((m, m), 1)
    return jnp.sum(jnp.where(same, jnp.broadcast_to(row, (m, m)), 0.0), axis=1, keepdims=True)


def flat_row(x, first, width):
    peers, slots = x.shape
    lane = iota((slots, width), 1)
    hot = (lane % slots == iota((slots, width), 0)).astype(f32)
    wide = pick_dot(x, hot)
    mine = (iota((peers, width), 1) + first) // slots == iota((peers, width), 0)
    return jnp.sum(jnp.where(mine, wide, 0.0), axis=0, keepdims=True)


def slot_of(dx, dy):
    return (dx + 1) * 3 + dy + 1


def kernel(
    n_gx, n_gy,
    diff_ref, base_ref, couple_ref, rows_ref, cols_ref, dirs_ref,
    cell_ref, weight_ref, count_ref, gauge_ref, prec_ref,
    read_ref, hess_ref,
    pc, pt, pb, rc, rr, coef, gcoef, first_sc, pert, hum, pk, qb, rb, vr, load, grad,
    proj, rsb, agb,
    near_send, near_recv, own_send, own_recv, back_send, back_recv,
    rs_send, rs_recv, ag_send, ag_recv,
):
    gx, gy = lax.axis_index("gx"), lax.axis_index("gy")
    n = n_gx * n_gy
    me = gx * n_gy + gy
    height, breadth = diff_ref.shape
    n_dirs, modes_x, modes_y = dirs_ref.shape
    peers, slots = cell_ref.shape[2], cell_ref.shape[3]
    gauges = prec_ref.shape[2]
    entries = peers * slots
    width = min(entries, 128)
    chunks = entries // width
    ext = height + 2 * PAD
    half = breadth // 2
    meta_c, meta_r = 3 * height + modes_y, 4 * PAD

    rc[...] = jnp.zeros_like(rc)
    rr[...] = jnp.zeros_like(rr)
    vr[...] = jnp.zeros_like(vr)

    barrier = pltpu.get_barrier_semaphore()

    def greet(i, carry):
        t = lax.rem(me + i, n)
        pl.semaphore_signal(
            barrier, inc=1, device_id=(t // n_gy, lax.rem(t, n_gy)),
            device_id_type=pl.DeviceIdType.MESH,
        )
        return carry

    lax.fori_loop(1, n, greet, 0)

    live = iota((peers, slots), 1).astype(f32) < column(count_ref[0].astype(f32))
    factor = jnp.where(live, weight_ref[0, 0], 0.0)
    cells = cell_ref[0, 0]
    cell_x, cell_y = (cells // breadth).astype(f32), (cells % breadth).astype(f32)
    pt[...] = jnp.zeros_like(pt)
    pb[...] = jnp.zeros_like(pb)
    pc[meta_c : meta_c + 8, :] = jnp.zeros((8, breadth), f32)
    my_rows = []
    for c in range(chunks):
        trio = [flat_row(v, c * width, width) for v in (cell_x, cell_y, factor)]
        my_rows.append(trio)
        for k, row in enumerate(trio):
            at = 2 * k + c
            pc[meta_c + at : meta_c + at + 1, :width] = row
            pt[meta_r + at : meta_r + at + 1, :width] = row
            pb[meta_r + at : meta_r + at + 1, :width] = row
    for k, ref in enumerate((diff_ref, base_ref, couple_ref)):
        pc[k * height : (k + 1) * height, :] = ref[...]
        pt[k * PAD : (k + 1) * PAD, :] = ref[:PAD, :]
        pb[k * PAD : (k + 1) * PAD, :] = ref[height - PAD :, :]
    pt[3 * PAD : 4 * PAD, :modes_x] = rows_ref[:PAD, :]
    pb[3 * PAD : 4 * PAD, :modes_x] = rows_ref[height - PAD :, :]
    cols_t = turned(cols_ref[...])[:modes_y]
    pc[3 * height : 3 * height + modes_y, :] = cols_t

    pl.semaphore_wait(barrier, n - 1)

    def exists(dx, dy):
        ok = None
        for d, at, size in ((dx, gx, n_gx), (dy, gy, n_gy)):
            if d:
                here = at > 0 if d < 0 else at < size - 1
                ok = here if ok is None else jnp.logical_and(ok, here)
        return ok

    def near_ref(dx, dy):
        if dx == 0:
            return rc.at[(dy + 1) // 2]
        return rr.at[(dx + 1) // 2 * 3 + dy + 1]

    def near_copy(dx, dy):
        src = pc if dx == 0 else (pt if dx < 0 else pb)
        return pltpu.make_async_remote_copy(
            src_ref=src, dst_ref=near_ref(-dx, -dy),
            send_sem=near_send.at[slot_of(dx, dy)], recv_sem=near_recv.at[slot_of(-dx, -dy)],
            device_id=(gx + dx, gy + dy), device_id_type=pl.DeviceIdType.MESH,
        )

    sides = [(dx, dy) for dx in (0, -1, 1) for dy in (-1, 0, 1) if dx or dy]
    for dx, dy in sides:

        @pl.when(exists(dx, dy))
        def _(dx=dx, dy=dy):
            near_copy(dx, dy).start()

    for dx, dy in sides:

        @pl.when(exists(dx, dy))
        def _(dx=dx, dy=dy):
            near_copy(-dx, -dy).wait_recv()

    lane = iota((ext, breadth), 1)

    def joined(middle, right, left):
        return jnp.concatenate([middle, jnp.where(iota(right.shape, 1) < half, right, left)], axis=1)

    def extended(k, ref):
        tile = slice(k * PAD, (k + 1) * PAD)
        block = slice(k * height, (k + 1) * height)
        stack = lambda dy, mid: jnp.concatenate(
            [rr[dy + 1, tile, :], mid, rr[3 + dy + 1, tile, :]], axis=0
        )
        return joined(stack(0, ref[...]), stack(1, rc[1, block, :]), stack(-1, rc[0, block, :]))

    diff = extended(0, diff_ref)
    base = extended(1, base_ref)
    couple = extended(2, couple_ref)
    row_at, lane_at = iota((ext, 2 * breadth), 0), iota((ext, 2 * breadth), 1)
    out_row = jnp.logical_or(
        jnp.logical_and(row_at < PAD, gx == 0),
        jnp.logical_and(row_at >= PAD + height, gx == n_gx - 1),
    )
    out_col = jnp.logical_or(
        jnp.logical_and(
            jnp.logical_and(lane_at >= breadth, lane_at < breadth + half), gy == n_gy - 1
        ),
        jnp.logical_and(lane_at >= breadth + half, gy == 0),
    )
    inside = jnp.where(jnp.logical_or(out_row, out_col), 0.0, 1.0).astype(f32)
    centre = inside
    s_sum = jnp.zeros_like(diff)
    own = (slice(PAD, PAD + height), slice(0, breadth))
    for k, (d_near, b_near) in enumerate(zip(around(diff), around(base))):
        weight = (step_ratio * 0.5) * (diff + d_near) * inside
        coef[1 + k] = weight
        centre = centre - weight
        gap = 0.5 * (b_near - base)
        gcoef[k] = (diff * gap)[own]
        pull = step_ratio * gap * inside
        coef[9 + k] = pull
        s_sum = s_sum + pull
    coef[0] = centre
    coef[5] = step_ratio * inside
    coef[6] = couple
    coef[7] = diff
    coef[8] = s_sum

    rows_ext = jnp.concatenate(
        [rr[1, 3 * PAD : 4 * PAD, :modes_x], rows_ref[...], rr[4, 3 * PAD : 4 * PAD, :modes_x]],
        axis=0,
    )
    own_cols = slice(3 * height, 3 * height + modes_y)
    cols_ext = joined(cols_t, rc[1, own_cols, :], rc[0, own_cols, :])
    for r in range(n_dirs):
        first_sc[r * ext : (r + 1) * ext, :] = dot(rows_ext, dirs_ref[r])
    pert[...] = dot(first_sc[...], cols_ext).reshape(n_dirs, ext, 2 * breadth)

    def stencil(t, h, sign):
        t_near, h_near = around(t), around(h)
        mixed = coef[0] * h
        total = t
        for k in range(4):
            mixed = mixed + coef[1 + k] * h_near[k]
            total = total + t_near[k]
        if sign > 0:
            return coef[5] * total + coef[6] * h, mixed - coef[6] * t
        return coef[5] * total - coef[6] * h, mixed + coef[6] * t

    def tangent(r, carry):
        p = coef[7] * pert[r]
        source = coef[8] * p
        for k, p_near in enumerate(around(p)):
            source = source + coef[9 + k] * p_near
        t, h = coef[6] * source, coef[0] * source
        for k, s_near in enumerate(around(source)):
            h = h + coef[1 + k] * s_near
        h = h + source
        for _ in range(STEPS - 2):
            t, h = stencil(t, h, 1)
            h = h + source
        hum[r] = h[own]
        return carry

    lax.fori_loop(0, n_dirs, tangent, 0)

    humid = hum[...].reshape(n_dirs * height, breadth)
    for c in range(chunks):
        x_row, y_row, f_row = my_rows[c]
        hot = (iota((breadth, width), 0).astype(f32) == y_row).astype(f32)
        picked = pick_dot(humid, hot).reshape(n_dirs, height, width)
        mine = jnp.where(iota((height, width), 0).astype(f32) == x_row, f_row, 0.0)
        picked = jnp.sum(picked * mine[None], axis=1)
        some = width // slots
        pk[c * some : (c + 1) * some] = turned(picked)[:width].reshape(some, slots, 128)

    def to_owner(o, slot):
        return pltpu.make_async_remote_copy(
            src_ref=pk.at[o], dst_ref=qb.at[slot], send_sem=own_send, recv_sem=own_recv,
            device_id=(o, gy), device_id_type=pl.DeviceIdType.MESH,
        )

    def send_picks(i, carry):
        to_owner(lax.rem(gx + i, n_gx), gx).start()
        return carry

    lax.fori_loop(1, n_gx, send_picks, 0)
    qb[gx] = pk[gx]
    gauge_f = gauge_ref[0, 0].astype(f32)
    hots = []
    for c in range(chunks):
        g_row = flat_row(gauge_f, c * width, width)
        hots.append((iota((128, width), 0).astype(f32) == g_row).astype(f32))
    prec = column(prec_ref[0])
    prec = jnp.concatenate([prec, jnp.zeros((128 - gauges, 1), f32)], axis=0)
    others = pl.ds(0, n_gx - 1)
    everyone = pltpu.make_async_remote_copy(
        src_ref=pk.at[others], dst_ref=qb.at[others], send_sem=own_send, recv_sem=own_recv,
        device_id=(gx, gy), device_id_type=pl.DeviceIdType.MESH,
    )
    everyone.wait_recv()
    some = width // slots
    gauge_read = jnp.zeros((128, 128), f32)
    for c in range(chunks):
        got = qb[c * some : (c + 1) * some].reshape(width, 128)
        gauge_read = gauge_read + dot(hots[c], got)
    weighted = gauge_read * prec
    rb[0] = jnp.zeros((slots, 128), f32)
    rb[n_gx + 1] = jnp.zeros((slots, 128), f32)
    for c in range(chunks):
        back = dot(turned(hots[c])[:width], weighted)
        rb[1 + c * some : 1 + (c + 1) * some] = back.reshape(some, slots, 128)

    def back_copy(t, dy):
        return pltpu.make_async_remote_copy(
            src_ref=rb.at[pl.ds(t, 3)], dst_ref=vr.at[1 - dy, :, gx],
            send_sem=back_send.at[1 + dy], recv_sem=back_recv.at[1 - dy],
            device_id=(t, gy + dy), device_id_type=pl.DeviceIdType.MESH,
        )

    def send_back(i, carry):
        t = lax.rem(gx + i, n_gx)
        for dy in (-1, 1):

            @pl.when(exists(0, dy))
            def _(dy=dy):
                back_copy(t, dy).start()

        @pl.when(i > 0)
        def _():
            back_copy(t, 0).start()

        return carry

    lax.fori_loop(0, n_gx, send_back, 0)
    vr[1, :, gx] = rb[pl.ds(gx, 3)]
    read_ref[0, 0] = gauge_read.T[:n_dirs, :gauges]

    def back_all(dy):
        span = pl.ds(0, n_gx if dy else n_gx - 1)
        return pltpu.make_async_remote_copy(
            src_ref=vr.at[1 + dy, :, span], dst_ref=vr.at[1 + dy, :, span],
            send_sem=back_send.at[1 + dy], recv_sem=back_recv.at[1 + dy],
            device_id=(gx, gy), device_id_type=pl.DeviceIdType.MESH,
        )

    back_all(0).wait_recv()
    for dy in (-1, 1):

        @pl.when(exists(0, dy))
        def _(dy=dy):
            back_all(dy).wait_recv()

    def meta_row(dx, dy, k, c):
        if dx == 0 and dy == 0:
            return my_rows[c][k]
        at = 2 * k + c
        if dx == 0:
            return rc[(dy + 1) // 2, meta_c + at : meta_c + at + 1, :width]
        return rr[(dx + 1) // 2 * 3 + dy + 1, meta_r + at : meta_r + at + 1, :width]

    for dx, at, first, tall in ((-1, 0, height - PAD, PAD), (0, PAD, 0, height), (1, PAD + height, 0, PAD)):
        parts = [None, None]
        for dy in (-1, 0, 1):
            for c in range(chunks):
                x_row, y_row, f_row = (meta_row(dx, dy, k, c) for k in range(3))
                got = vr[dy + 1, dx + 1, c * some : (c + 1) * some].reshape(width, 128)
                values = turned(got)[:n_dirs, :width] * f_row
                hit_x = (iota((tall, width), 0) + first).astype(f32) == x_row
                y_at = iota((breadth, width), 0)
                hit_y = y_at.astype(f32) == y_row
                if dy:
                    hit_y = jnp.logical_and(hit_y, y_at < half if dy > 0 else y_at >= half)
                spread_x = jnp.where(hit_x[None], values[:, None, :], 0.0)
                term = pick_dot(
                    spread_x.reshape(n_dirs * tall, width), hit_y.astype(f32), NT
                )
                tile = 1 if dy else 0
                parts[tile] = term if parts[tile] is None else parts[tile] + term
        for tile in (0, 1):
            load[:, at : at + tall, tile * breadth : (tile + 1) * breadth] = parts[tile].reshape(
                n_dirs, tall, breadth
            )

    group = 128 // modes_y

    def adjoint(r, carry):
        b = load[r]
        summed = b
        a, b = -(coef[6] * b), coef[0] * b
        for k, l_near in enumerate(around(summed)):
            b = b + coef[1 + k] * l_near
        summed = summed + b
        for _ in range(STEPS - 2):
            a, b = stencil(a, b, -1)
            summed = summed + b
        lam = step_ratio * summed
        total = None
        for k, l_near in enumerate(around(lam)):
            term = gcoef[k] * (lam[own] - l_near[own])
            total = term if total is None else total + term
        grad[lax.rem(r, group), r // group] = total
        return carry

    lax.fori_loop(0, n_dirs, adjoint, 0)

    quads = n_dirs // group
    half_way = None
    for j in range(group):
        pieces = []
        if j:
            pieces.append(jnp.zeros((j * modes_y, breadth), f32))
        pieces.append(cols_t)
        if j < group - 1:
            pieces.append(jnp.zeros(((group - 1 - j) * modes_y, breadth), f32))
        placed = jnp.concatenate(pieces, axis=0)
        term = dot(grad[j].reshape(quads * height, breadth), placed, NT)
        half_way = term if half_way is None else half_way + term
    rows_t = turned(rows_ref[...])[:modes_x, :height]
    size = proj.shape[1]
    per = modes_x // size
    for q in range(quads):
        both = dot(rows_t, half_way[q * height : (q + 1) * height])
        if per:
            proj[q * per : (q + 1) * per] = both.reshape(per, size, 128)
        else:
            ratio = size // modes_x
            proj[q // ratio, (q % ratio) * modes_x : (q % ratio + 1) * modes_x] = both

    owners = proj.shape[0]

    def share(t):
        return pltpu.make_async_remote_copy(
            src_ref=proj.at[t], dst_ref=rsb.at[me], send_sem=rs_send, recv_sem=rs_recv,
            device_id=(t // n_gy, lax.rem(t, n_gy)), device_id_type=pl.DeviceIdType.MESH,
        )

    def result(t):
        return pltpu.make_async_remote_copy(
            src_ref=agb.at[me], dst_ref=agb.at[me], send_sem=ag_send, recv_sem=ag_recv,
            device_id=(t // n_gy, lax.rem(t, n_gy)), device_id_type=pl.DeviceIdType.MESH,
        )

    def waiter(ref, count, send, recv):
        span = ref.at[pl.ds(0, count)]
        return pltpu.make_async_remote_copy(
            src_ref=span, dst_ref=span, send_sem=send, recv_sem=recv,
            device_id=(gx, gy), device_id_type=pl.DeviceIdType.MESH,
        )

    def send_share(i, carry):
        t = lax.rem(me + i, n)
        if owners == n:
            share(t).start()
        else:

            @pl.when(t < owners)
            def _():
                share(t).start()

        return carry

    lax.fori_loop(1, n, send_share, 0)

    def own_part():
        rsb[me] = proj[me]
        waiter(rsb, n - 1, rs_send, rs_recv).wait_recv()
        agb[me] = jnp.sum(rsb[...], axis=0)

        def send_result(i, carry):
            result(lax.rem(me + i, n)).start()
            return carry

        lax.fori_loop(1, n, send_result, 0)
        if owners > 1:
            waiter(agb, owners - 1, ag_send, ag_recv).wait_recv()
        waiter(rsb, n - 1, ag_send, ag_recv).wait_send()
        if owners > 1:
            waiter(agb, owners - 1, rs_send, rs_recv).wait_send()

    def other_part():
        waiter(agb, owners, ag_send, ag_recv).wait_recv()
        waiter(agb, owners, rs_send, rs_recv).wait_send()

    if owners == n:
        own_part()
    else:
        pl.when(me < owners)(own_part)
        pl.when(me >= owners)(other_part)

    summed = agb[...].reshape(quads, modes_x, 128)
    for r in range(n_dirs):
        q, j = r // group, r % group
        hess_ref[r] = dirs_ref[r] + summed[q][:, j * modes_y : (j + 1) * modes_y]

    for dx, dy in sides:

        @pl.when(exists(dx, dy))
        def _(dx=dx, dy=dy):
            near_copy(dx, dy).wait_send()

    everyone.wait_send()
    back_all(0).wait_send()
    for dy in (-1, 1):

        @pl.when(exists(0, dy))
        def _(dy=dy):
            back_all(dy).wait_send()


def local(n_gx, n_gy, *args):
    diffusivity, dirs, cells, noise = args[0], args[5], args[6], args[10]
    height, breadth = diffusivity.shape
    n_dirs, modes_x, modes_y = dirs.shape
    peers, slots = cells.shape[2], cells.shape[3]
    gauges = noise.shape[2]
    n = n_gx * n_gy
    ext = height + 2 * PAD
    total_rows = n_dirs * modes_x * modes_y // 128
    size = max(8, total_rows // n)
    owners = total_rows // size
    group = 128 // modes_y
    vmem = lambda *shape: pltpu.VMEM(shape, f32)
    dma = pltpu.SemaphoreType.DMA
    space = pl.BlockSpec(memory_space=pltpu.VMEM)
    return pl.pallas_call(
        functools.partial(kernel, n_gx, n_gy),
        out_shape=(
            jax.ShapeDtypeStruct((1, 1, n_dirs, gauges), f32),
            jax.ShapeDtypeStruct(dirs.shape, f32),
        ),
        in_specs=[space] * len(args),
        out_specs=(space, space),
        scratch_shapes=[
            vmem(3 * height + modes_y + 8, breadth),
            vmem(5 * PAD, breadth),
            vmem(5 * PAD, breadth),
            vmem(2, 3 * height + modes_y + 8, breadth),
            vmem(6, 5 * PAD, breadth),
            vmem(13, ext, 2 * breadth),
            vmem(4, height, breadth),
            vmem(n_dirs * ext, modes_y),
            vmem(n_dirs, ext, 2 * breadth),
            vmem(n_dirs, height, breadth),
            vmem(peers, slots, 128),
            vmem(peers, slots, 128),
            vmem(peers + 2, slots, 128),
            vmem(3, 3, peers, slots, 128),
            vmem(n_dirs, ext, 2 * breadth),
            vmem(group, n_dirs // group, height, breadth),
            vmem(owners, size, 128),
            vmem(n, size, 128),
            vmem(owners, size, 128),
            dma((9,)),
            dma((9,)),
            dma,
            dma,
            dma((3,)),
            dma((3,)),
            dma,
            dma,
            dma,
            dma,
        ],
        compiler_params=pltpu.CompilerParams(
            collective_id=0, has_side_effects=True, vmem_limit_bytes=40 * 1024 * 1024
        ),
    )(*args)


def solution(mesh):
    placed = (
        P("gx", "gy"),
        P("gx", "gy"),
        P("gx", "gy"),
        P("gx", None),
        P("gy", None),
        P(),
        P("gx", "gy", None, None),
        P("gx", "gy", None, None),
        P("gx", "gy", None),
        P("gx", "gy", None, None),
        P("gx", "gy", None),
    )
    return jax.shard_map(
        functools.partial(local, mesh.shape["gx"], mesh.shape["gy"]),
        mesh=mesh,
        in_specs=placed,
        out_specs=(P("gx", "gy", None, None), P()),
        check_vma=False,
    )
```

```python
import functools

import jax
import jax.numpy as jnp
from jax import lax
from jax.experimental import pallas as pl
from jax.experimental.pallas import tpu as pltpu
from jax.sharding import PartitionSpec as P

STEPS = 6
step_ratio = 0.2
exact = lax.Precision.HIGHEST
f32 = jnp.float32
bf16 = jnp.bfloat16
PAD = 8
BLOCK = 2
UNROLL = 2
NN = (((1,), (0,)), ((), ()))
NT = (((1,), (1,)), ((), ()))


def iota(shape, dim):
    return lax.broadcasted_iota(jnp.int32, shape, dim)


def dot(a, b, dims=NN):
    return lax.dot_general(a, b, dims, precision=exact, preferred_element_type=f32)


def pick_dot(values, hot, dims=NN):
    hot = hot.astype(bf16)
    total = None
    for _ in range(3):
        part = values.astype(bf16)
        values = values - part.astype(f32)
        term = lax.dot_general(part, hot, dims, preferred_element_type=f32)
        total = term if total is None else total + term
    return total


def around(v):
    rows, cols = v.shape
    return (
        pltpu.roll(v, 1, 0),
        pltpu.roll(v, rows - 1, 0),
        pltpu.roll(v, 1, 1),
        pltpu.roll(v, cols - 1, 1),
    )


def turned(v):
    rows, cols = v.shape
    if cols % 128:
        v = jnp.concatenate([v, jnp.zeros((rows, 128 - cols % 128), f32)], axis=1)
    if rows % 128:
        v = jnp.concatenate([v, jnp.zeros((128 - rows % 128, v.shape[1]), f32)], axis=0)
    return v.T


def column(row):
    m = row.shape[1]
    same = iota((m, m), 0) == iota((m, m), 1)
    return jnp.sum(jnp.where(same, jnp.broadcast_to(row, (m, m)), 0.0), axis=1, keepdims=True)


def flat_row(x, first, width):
    peers, slots = x.shape
    lane = iota((slots, width), 1)
    hot = (lane % slots == iota((slots, width), 0)).astype(f32)
    wide = pick_dot(x, hot)
    mine = (iota((peers, width), 1) + first) // slots == iota((peers, width), 0)
    return jnp.sum(jnp.where(mine, wide, 0.0), axis=0, keepdims=True)


def keep(ref, k, v):
    ref[k] = jnp.broadcast_to(v[:, None, :], (v.shape[0], 8, v.shape[1]))


def slot_of(dx, dy):
    return (dx + 1) * 3 + dy + 1


def kernel(
    n_gx, n_gy,
    diff_ref, base_ref, couple_ref, rows_ref, cols_ref, dirs_ref,
    cell_ref, weight_ref, count_ref, gauge_ref, prec_ref,
    read_ref, hess_ref,
    pc, pt, pb, rc, rr, coef, gcoef, first_sc, pert, ta, ha, tb, hb, pk, qb, rb, vr, load, grad,
    proj, rsb, agb,
    near_send, near_recv, own_send, own_recv, back_send, back_recv,
    rs_send, rs_recv, ag_send, ag_recv,
):
    gx, gy = lax.axis_index("gx"), lax.axis_index("gy")
    n = n_gx * n_gy
    me = gx * n_gy + gy
    height, breadth = diff_ref.shape
    n_dirs, modes_y, modes_x = dirs_ref.shape
    peers, slots = cell_ref.shape[2], cell_ref.shape[3]
    gauges = prec_ref.shape[2]
    entries = peers * slots
    width = min(entries, 128)
    chunks = entries // width
    ext = height + 2 * PAD
    half = breadth // 2
    meta_c, meta_r = 3 * height + modes_y, 4 * PAD

    rc[...] = jnp.zeros_like(rc)
    rr[...] = jnp.zeros_like(rr)
    vr[...] = jnp.zeros_like(vr)

    barrier = pltpu.get_barrier_semaphore()

    def greet(i, carry):
        t = lax.rem(me + i, n)
        pl.semaphore_signal(
            barrier, inc=1, device_id=(t // n_gy, lax.rem(t, n_gy)),
            device_id_type=pl.DeviceIdType.MESH,
        )
        return carry

    lax.fori_loop(1, n, greet, 0)

    live = iota((peers, slots), 1).astype(f32) < column(count_ref[0].astype(f32))
    factor = jnp.where(live, weight_ref[0, 0], 0.0)
    cells = cell_ref[0, 0]
    cell_x, cell_y = (cells // breadth).astype(f32), (cells % breadth).astype(f32)
    pt[...] = jnp.zeros_like(pt)
    pb[...] = jnp.zeros_like(pb)
    pc[meta_c : meta_c + 8, :] = jnp.zeros((8, breadth), f32)
    my_rows = []
    for c in range(chunks):
        trio = [flat_row(v, c * width, width) for v in (cell_x, cell_y, factor)]
        my_rows.append(trio)
        for k, row in enumerate(trio):
            at = 2 * k + c
            pc[meta_c + at : meta_c + at + 1, :width] = row
            pt[meta_r + at : meta_r + at + 1, :width] = row
            pb[meta_r + at : meta_r + at + 1, :width] = row
    for k, ref in enumerate((diff_ref, base_ref, couple_ref)):
        pc[k * height : (k + 1) * height, :] = ref[...]
        pt[k * PAD : (k + 1) * PAD, :] = ref[:PAD, :]
        pb[k * PAD : (k + 1) * PAD, :] = ref[height - PAD :, :]
    pt[3 * PAD : 4 * PAD, :modes_x] = rows_ref[:PAD, :]
    pb[3 * PAD : 4 * PAD, :modes_x] = rows_ref[height - PAD :, :]
    cols_t = cols_ref[...]
    pc[3 * height : 3 * height + modes_y, :] = cols_t

    pl.semaphore_wait(barrier, n - 1)

    def exists(dx, dy):
        ok = None
        for d, at, size in ((dx, gx, n_gx), (dy, gy, n_gy)):
            if d:
                here = at > 0 if d < 0 else at < size - 1
                ok = here if ok is None else jnp.logical_and(ok, here)
        return ok

    def near_ref(dx, dy):
        if dx == 0:
            return rc.at[(dy + 1) // 2]
        return rr.at[(dx + 1) // 2 * 3 + dy + 1]

    def near_copy(dx, dy):
        src = pc if dx == 0 else (pt if dx < 0 else pb)
        return pltpu.make_async_remote_copy(
            src_ref=src, dst_ref=near_ref(-dx, -dy),
            send_sem=near_send.at[slot_of(dx, dy)], recv_sem=near_recv.at[slot_of(-dx, -dy)],
            device_id=(gx + dx, gy + dy), device_id_type=pl.DeviceIdType.MESH,
        )

    sides = [(dx, dy) for dx in (0, -1, 1) for dy in (-1, 0, 1) if dx or dy]
    for dx, dy in sides:

        @pl.when(exists(dx, dy))
        def _(dx=dx, dy=dy):
            near_copy(dx, dy).start()

    for dx, dy in sides:

        @pl.when(exists(dx, dy))
        def _(dx=dx, dy=dy):
            near_copy(-dx, -dy).wait_recv()

    lane = iota((ext, breadth), 1)

    def joined(middle, right, left):
        return jnp.concatenate([middle, jnp.where(iota(right.shape, 1) < half, right, left)], axis=1)

    def extended(k, ref):
        tile = slice(k * PAD, (k + 1) * PAD)
        block = slice(k * height, (k + 1) * height)
        stack = lambda dy, mid: jnp.concatenate(
            [rr[dy + 1, tile, :], mid, rr[3 + dy + 1, tile, :]], axis=0
        )
        return joined(stack(0, ref[...]), stack(1, rc[1, block, :]), stack(-1, rc[0, block, :]))

    diff = extended(0, diff_ref)
    base = extended(1, base_ref)
    couple = extended(2, couple_ref)
    row_at, lane_at = iota((ext, 2 * breadth), 0), iota((ext, 2 * breadth), 1)
    out_row = jnp.logical_or(
        jnp.logical_and(row_at < PAD, gx == 0),
        jnp.logical_and(row_at >= PAD + height, gx == n_gx - 1),
    )
    out_col = jnp.logical_or(
        jnp.logical_and(
            jnp.logical_and(lane_at >= breadth, lane_at < breadth + half), gy == n_gy - 1
        ),
        jnp.logical_and(lane_at >= breadth + half, gy == 0),
    )
    inside = jnp.where(jnp.logical_or(out_row, out_col), 0.0, 1.0).astype(f32)
    centre = inside
    s_sum = jnp.zeros_like(diff)
    own = (slice(PAD, PAD + height), slice(0, breadth))
    for k, (d_near, b_near) in enumerate(zip(around(diff), around(base))):
        weight = (step_ratio * 0.5) * (diff + d_near) * inside
        keep(coef, 1 + k, weight)
        centre = centre - weight
        gap = 0.5 * (b_near - base)
        keep(gcoef, k, (diff * gap)[own])
        pull = step_ratio * gap * inside
        keep(coef, 9 + k, pull)
        s_sum = s_sum + pull
    keep(coef, 0, centre)
    keep(coef, 5, step_ratio * inside)
    keep(coef, 6, couple)
    keep(coef, 7, diff)
    keep(coef, 8, s_sum)

    rows_ext = jnp.concatenate(
        [rr[1, 3 * PAD : 4 * PAD, :modes_x], rows_ref[...], rr[4, 3 * PAD : 4 * PAD, :modes_x]],
        axis=0,
    )
    own_cols = slice(3 * height, 3 * height + modes_y)
    cols_ext = joined(cols_t, rc[1, own_cols, :], rc[0, own_cols, :])
    group = 128 // modes_y
    quads = n_dirs // group
    lane_group = iota((ext, 128), 1) // modes_y
    for q in range(quads):
        block = dirs_ref[q * group : (q + 1) * group].reshape(128, modes_x)
        both = dot(rows_ext, block, NT)
        for j in range(group):
            rows = pl.ds(q * group + j, ext, stride=n_dirs)
            first_sc[rows, :] = jnp.where(lane_group == j, both, 0.0)
    stacked = jnp.concatenate([cols_ext] * group, axis=0)
    wide = (ext, n_dirs, 2 * breadth)

    def perturb(i, carry):
        rows = pl.ds(pl.multiple_of(i * 8 * n_dirs, 8 * n_dirs), 8 * n_dirs)
        pert[pl.ds(i * 8, 8)] = dot(first_sc[rows, :], stacked).reshape((8,) + wide[1:])
        return carry

    lax.fori_loop(0, ext // 8, perturb, 0)

    def sides_of(v):
        size = v.shape[-1]
        return pltpu.roll(v, 1, 2), pltpu.roll(v, size - 1, 2)

    def near_of(ref, x, middle):
        return (ref[pl.ds(x - 1, BLOCK)], ref[pl.ds(x + 1, BLOCK)]) + sides_of(middle)

    def times(k, x, v):
        c = coef[k, pl.ds(x, BLOCK)]
        return jnp.concatenate(
            [c * v[:, g * 8 : (g + 1) * 8] for g in range(n_dirs // 8)], axis=1
        )

    def over_rows(margin, body):
        step = BLOCK * UNROLL
        count = -(-(height + 2 * margin) // step)

        def several(i, carry):
            for u in range(UNROLL):
                body(PAD - margin + i * step + u * BLOCK)
            return carry

        lax.fori_loop(0, count, several, 0)

    def mixed_with(x, h, ref):
        total = times(0, x, h)
        for k, near in enumerate(near_of(ref, x, h)):
            total = total + times(1 + k, x, near)
        return total

    def stencil(x, t_old, h_old, sign):
        t, h = t_old[pl.ds(x, BLOCK)], h_old[pl.ds(x, BLOCK)]
        total = t
        for near in near_of(t_old, x, t):
            total = total + near
        mixed = mixed_with(x, h, h_old)
        if sign > 0:
            return times(5, x, total) + times(6, x, h), mixed - times(6, x, t)
        return times(5, x, total) - times(6, x, h), mixed + times(6, x, t)

    def scaled(x):
        rows = pl.ds(x, BLOCK)
        load[rows] = times(7, x, pert[rows])

    over_rows(STEPS, scaled)

    def make_source(x):
        rows = pl.ds(x, BLOCK)
        p = load[rows]
        total = times(8, x, p)
        for k, near in enumerate(near_of(load, x, p)):
            total = total + times(9 + k, x, near)
        pert[rows] = total

    over_rows(STEPS - 1, make_source)

    pairs = ((ta, ha), (tb, hb))

    def first_step(x):
        rows = pl.ds(x, BLOCK)
        source = pert[rows]
        ta[rows] = times(6, x, source)
        ha[rows] = mixed_with(x, source, pert) + source

    over_rows(STEPS - 2, first_step)
    for i in range(STEPS - 2):
        (t_old, h_old), (t_new, h_new) = pairs[i % 2], pairs[(i + 1) % 2]

        def next_step(x, t_old=t_old, h_old=h_old, t_new=t_new, h_new=h_new):
            rows = pl.ds(x, BLOCK)
            t, h = stencil(x, t_old, h_old, 1)
            t_new[rows] = t
            h_new[rows] = h + pert[rows]

        over_rows(STEPS - 3 - i, next_step)
    hum = pairs[(STEPS - 2) % 2][1]

    humid = hum[PAD : PAD + height, :, :breadth].reshape(height * n_dirs, breadth)
    for c in range(chunks):
        x_row, y_row, f_row = my_rows[c]
        hot = (iota((breadth, width), 0).astype(f32) == y_row).astype(f32)
        picked = pick_dot(humid, hot).reshape(height, n_dirs, width)
        at_x = iota(picked.shape, 0).astype(f32) == x_row[None]
        picked = jnp.sum(jnp.where(at_x, picked, 0.0), axis=0) * f_row
        some = width // slots
        pk[c * some : (c + 1) * some] = turned(picked)[:width].reshape(some, slots, 128)

    def to_owner(o, slot):
        return pltpu.make_async_remote_copy(
            src_ref=pk.at[o], dst_ref=qb.at[slot], send_sem=own_send, recv_sem=own_recv,
            device_id=(o, gy), device_id_type=pl.DeviceIdType.MESH,
        )

    def send_picks(i, carry):
        to_owner(lax.rem(gx + i, n_gx), gx).start()
        return carry

    lax.fori_loop(1, n_gx, send_picks, 0)
    qb[gx] = pk[gx]
    gauge_f = gauge_ref[0, 0].astype(f32)
    hots = []
    for c in range(chunks):
        g_row = flat_row(gauge_f, c * width, width)
        hots.append((iota((128, width), 0).astype(f32) == g_row).astype(f32))
    prec = column(prec_ref[0])
    prec = jnp.concatenate([prec, jnp.zeros((128 - gauges, 1), f32)], axis=0)
    others = pl.ds(0, n_gx - 1)
    everyone = pltpu.make_async_remote_copy(
        src_ref=pk.at[others], dst_ref=qb.at[others], send_sem=own_send, recv_sem=own_recv,
        device_id=(gx, gy), device_id_type=pl.DeviceIdType.MESH,
    )
    everyone.wait_recv()
    some = width // slots
    gauge_read = jnp.zeros((128, 128), f32)
    for c in range(chunks):
        got = qb[c * some : (c + 1) * some].reshape(width, 128)
        gauge_read = gauge_read + dot(hots[c], got)
    weighted = gauge_read * prec
    rb[0] = jnp.zeros((slots, 128), f32)
    rb[n_gx + 1] = jnp.zeros((slots, 128), f32)
    for c in range(chunks):
        back = dot(turned(hots[c])[:width], weighted)
        rb[1 + c * some : 1 + (c + 1) * some] = back.reshape(some, slots, 128)

    def back_copy(t, dy):
        return pltpu.make_async_remote_copy(
            src_ref=rb.at[pl.ds(t, 3)], dst_ref=vr.at[1 - dy, :, gx],
            send_sem=back_send.at[1 + dy], recv_sem=back_recv.at[1 - dy],
            device_id=(t, gy + dy), device_id_type=pl.DeviceIdType.MESH,
        )

    def send_back(i, carry):
        t = lax.rem(gx + i, n_gx)
        for dy in (-1, 1):

            @pl.when(exists(0, dy))
            def _(dy=dy):
                back_copy(t, dy).start()

        @pl.when(i > 0)
        def _():
            back_copy(t, 0).start()

        return carry

    lax.fori_loop(0, n_gx, send_back, 0)
    vr[1, :, gx] = rb[pl.ds(gx, 3)]
    read_ref[0, 0] = gauge_read.T[:n_dirs, :gauges]

    def back_all(dy):
        span = pl.ds(0, n_gx if dy else n_gx - 1)
        return pltpu.make_async_remote_copy(
            src_ref=vr.at[1 + dy, :, span], dst_ref=vr.at[1 + dy, :, span],
            send_sem=back_send.at[1 + dy], recv_sem=back_recv.at[1 + dy],
            device_id=(gx, gy), device_id_type=pl.DeviceIdType.MESH,
        )

    back_all(0).wait_recv()
    for dy in (-1, 1):

        @pl.when(exists(0, dy))
        def _(dy=dy):
            back_all(dy).wait_recv()

    def meta_row(dx, dy, k, c):
        if dx == 0 and dy == 0:
            return my_rows[c][k]
        at = 2 * k + c
        if dx == 0:
            return rc[(dy + 1) // 2, meta_c + at : meta_c + at + 1, :width]
        return rr[(dx + 1) // 2 * 3 + dy + 1, meta_r + at : meta_r + at + 1, :width]

    for dx, at, first, tall in ((-1, 0, height - PAD, PAD), (0, PAD, 0, height), (1, PAD + height, 0, PAD)):
        parts = [None, None]
        for dy in (-1, 0, 1):
            for c in range(chunks):
                x_row, y_row, f_row = (meta_row(dx, dy, k, c) for k in range(3))
                got = vr[dy + 1, dx + 1, c * some : (c + 1) * some].reshape(width, 128)
                values = turned(got)[:n_dirs, :width] * f_row
                at_x = (iota((tall, n_dirs, width), 0) + first).astype(f32) == x_row[None]
                y_at = iota((breadth, width), 0)
                hit_y = y_at.astype(f32) == y_row
                if dy:
                    hit_y = jnp.logical_and(hit_y, y_at < half if dy > 0 else y_at >= half)
                spread_x = jnp.where(at_x, values[None], 0.0)
                term = pick_dot(
                    spread_x.reshape(tall * n_dirs, width), hit_y.astype(f32), NT
                )
                tile = 1 if dy else 0
                parts[tile] = term if parts[tile] is None else parts[tile] + term
        for tile in (0, 1):
            load[at : at + tall, :, tile * breadth : (tile + 1) * breadth] = parts[tile].reshape(
                tall, n_dirs, breadth
            )

    def first_back(x):
        rows = pl.ds(x, BLOCK)
        b = load[rows]
        ta[rows] = -times(6, x, b)
        b_new = mixed_with(x, b, load)
        ha[rows] = b_new
        pert[rows] = b + b_new

    over_rows(STEPS - 1, first_back)
    for i in range(STEPS - 2):
        (t_old, h_old), (t_new, h_new) = pairs[i % 2], pairs[(i + 1) % 2]

        def next_back(x, t_old=t_old, h_old=h_old, t_new=t_new, h_new=h_new):
            rows = pl.ds(x, BLOCK)
            t, h = stencil(x, t_old, h_old, -1)
            t_new[rows] = t
            h_new[rows] = h
            pert[rows] = pert[rows] + h

        over_rows(STEPS - 2 - i, next_back)

    def gradient(x):
        lam = pert[pl.ds(x, BLOCK)]
        total = None
        for k, near in enumerate(near_of(pert, x, lam)):
            gap = step_ratio * (lam - near)[:, :, :breadth]
            c = gcoef[k, pl.ds(x - PAD, BLOCK)]
            term = jnp.concatenate(
                [c * gap[:, g * 8 : (g + 1) * 8] for g in range(n_dirs // 8)], axis=1
            )
            total = term if total is None else total + term
        start = (x - PAD) * n_dirs
        grad[pl.ds(pl.multiple_of(start, 8), BLOCK * n_dirs), :] = total.reshape(
            BLOCK * n_dirs, breadth
        )

    over_rows(0, gradient)

    half_way = None
    for j in range(group):
        pieces = []
        if j:
            pieces.append(jnp.zeros((j * modes_y, breadth), f32))
        pieces.append(cols_t)
        if j < group - 1:
            pieces.append(jnp.zeros(((group - 1 - j) * modes_y, breadth), f32))
        placed = jnp.concatenate(pieces, axis=0)
        mine = jnp.concatenate(
            [grad[pl.ds(q * group + j, height, stride=n_dirs), :] for q in range(quads)], axis=0
        )
        term = dot(mine, placed, NT)
        half_way = term if half_way is None else half_way + term
    rows_t = turned(rows_ref[...])[:modes_x, :height]
    size = proj.shape[1]
    per = modes_x // size
    for q in range(quads):
        both = dot(rows_t, half_way[q * height : (q + 1) * height])
        if per:
            proj[q * per : (q + 1) * per] = both.reshape(per, size, 128)
        else:
            ratio = size // modes_x
            proj[q // ratio, (q % ratio) * modes_x : (q % ratio + 1) * modes_x] = both

    owners = proj.shape[0]

    def share(t):
        return pltpu.make_async_remote_copy(
            src_ref=proj.at[t], dst_ref=rsb.at[me], send_sem=rs_send, recv_sem=rs_recv,
            device_id=(t // n_gy, lax.rem(t, n_gy)), device_id_type=pl.DeviceIdType.MESH,
        )

    def result(t):
        return pltpu.make_async_remote_copy(
            src_ref=agb.at[me], dst_ref=agb.at[me], send_sem=ag_send, recv_sem=ag_recv,
            device_id=(t // n_gy, lax.rem(t, n_gy)), device_id_type=pl.DeviceIdType.MESH,
        )

    def waiter(ref, count, send, recv):
        span = ref.at[pl.ds(0, count)]
        return pltpu.make_async_remote_copy(
            src_ref=span, dst_ref=span, send_sem=send, recv_sem=recv,
            device_id=(gx, gy), device_id_type=pl.DeviceIdType.MESH,
        )

    def send_share(i, carry):
        t = lax.rem(me + i, n)
        if owners == n:
            share(t).start()
        else:

            @pl.when(t < owners)
            def _():
                share(t).start()

        return carry

    lax.fori_loop(1, n, send_share, 0)

    def own_part():
        rsb[me] = proj[me]
        waiter(rsb, n - 1, rs_send, rs_recv).wait_recv()
        agb[me] = jnp.sum(rsb[...], axis=0)

        def send_result(i, carry):
            result(lax.rem(me + i, n)).start()
            return carry

        lax.fori_loop(1, n, send_result, 0)
        if owners > 1:
            waiter(agb, owners - 1, ag_send, ag_recv).wait_recv()
        waiter(rsb, n - 1, ag_send, ag_recv).wait_send()
        if owners > 1:
            waiter(agb, owners - 1, rs_send, rs_recv).wait_send()

    def other_part():
        waiter(agb, owners, ag_send, ag_recv).wait_recv()
        waiter(agb, owners, rs_send, rs_recv).wait_send()

    if owners == n:
        own_part()
    else:
        pl.when(me < owners)(own_part)
        pl.when(me >= owners)(other_part)

    summed = agb[...].reshape(quads, modes_x, 128)
    for q in range(quads):
        dirs = dirs_ref[q * group : (q + 1) * group]
        hess_ref[q * group : (q + 1) * group] = dirs + turned(summed[q])[:, :modes_x].reshape(
            dirs.shape
        )

    for dx, dy in sides:

        @pl.when(exists(dx, dy))
        def _(dx=dx, dy=dy):
            near_copy(dx, dy).wait_send()

    everyone.wait_send()
    back_all(0).wait_send()
    for dy in (-1, 1):

        @pl.when(exists(0, dy))
        def _(dy=dy):
            back_all(dy).wait_send()


def local(n_gx, n_gy, *args):
    args = list(args)
    args[4] = args[4].T
    args[5] = args[5].transpose(0, 2, 1)
    diffusivity, dirs, cells, noise = args[0], args[5], args[6], args[10]
    height, breadth = diffusivity.shape
    n_dirs, modes_y, modes_x = dirs.shape
    peers, slots = cells.shape[2], cells.shape[3]
    gauges = noise.shape[2]
    n = n_gx * n_gy
    ext = height + 2 * PAD
    total_rows = n_dirs * modes_x * modes_y // 128
    size = max(8, total_rows // n)
    owners = total_rows // size
    vmem = lambda *shape: pltpu.VMEM(shape, f32)
    dma = pltpu.SemaphoreType.DMA
    space = pl.BlockSpec(memory_space=pltpu.VMEM)
    readings, hess = pl.pallas_call(
        functools.partial(kernel, n_gx, n_gy),
        out_shape=(
            jax.ShapeDtypeStruct((1, 1, n_dirs, gauges), f32),
            jax.ShapeDtypeStruct(dirs.shape, f32),
        ),
        in_specs=[space] * len(args),
        out_specs=(space, space),
        scratch_shapes=[
            vmem(3 * height + modes_y + 8, breadth),
            vmem(5 * PAD, breadth),
            vmem(5 * PAD, breadth),
            vmem(2, 3 * height + modes_y + 8, breadth),
            vmem(6, 5 * PAD, breadth),
            vmem(13, ext, 8, 2 * breadth),
            vmem(4, height, 8, breadth),
            vmem(ext * n_dirs, 128),
            vmem(ext, n_dirs, 2 * breadth),
            vmem(ext, n_dirs, 2 * breadth),
            vmem(ext, n_dirs, 2 * breadth),
            vmem(ext, n_dirs, 2 * breadth),
            vmem(ext, n_dirs, 2 * breadth),
            vmem(peers, slots, 128),
            vmem(peers, slots, 128),
            vmem(peers + 2, slots, 128),
            vmem(3, 3, peers, slots, 128),
            vmem(ext, n_dirs, 2 * breadth),
            vmem(height * n_dirs, breadth),
            vmem(owners, size, 128),
            vmem(n, size, 128),
            vmem(owners, size, 128),
            dma((9,)),
            dma((9,)),
            dma,
            dma,
            dma((3,)),
            dma((3,)),
            dma,
            dma,
            dma,
            dma,
        ],
        compiler_params=pltpu.CompilerParams(
            collective_id=0, has_side_effects=True, vmem_limit_bytes=40 * 1024 * 1024
        ),
    )(*args)
    return readings, hess.transpose(0, 2, 1)


def solution(mesh):
    placed = (
        P("gx", "gy"),
        P("gx", "gy"),
        P("gx", "gy"),
        P("gx", None),
        P("gy", None),
        P(),
        P("gx", "gy", None, None),
        P("gx", "gy", None, None),
        P("gx", "gy", None),
        P("gx", "gy", None, None),
        P("gx", "gy", None),
    )
    return jax.shard_map(
        functools.partial(local, mesh.shape["gx"], mesh.shape["gy"]),
        mesh=mesh,
        in_specs=placed,
        out_specs=(P("gx", "gy", None, None), P()),
        check_vma=False,
    )
```

```python
import functools

import jax
import jax.numpy as jnp
from jax import lax
from jax.experimental import pallas as pl
from jax.experimental.pallas import tpu as pltpu
from jax.sharding import PartitionSpec as P

STEPS = 6
step_ratio = 0.2
exact = lax.Precision.HIGHEST
f32 = jnp.float32
bf16 = jnp.bfloat16
PAD = 8
N_IN = 11
BLOCK = 2
NN = (((1,), (0,)), ((), ()))
NT = (((1,), (1,)), ((), ()))


def iota(shape, dim):
    return lax.broadcasted_iota(jnp.int32, shape, dim)


def dot(a, b, dims=NN):
    return lax.dot_general(a, b, dims, precision=exact, preferred_element_type=f32)


def pick_dot(values, hot, dims=NN):
    hot = hot.astype(bf16)
    total = None
    for _ in range(3):
        part = values.astype(bf16)
        values = values - part.astype(f32)
        term = lax.dot_general(part, hot, dims, preferred_element_type=f32)
        total = term if total is None else total + term
    return total


def around(v):
    rows, cols = v.shape
    return (
        pltpu.roll(v, 1, 0),
        pltpu.roll(v, rows - 1, 0),
        pltpu.roll(v, 1, 1),
        pltpu.roll(v, cols - 1, 1),
    )


def turned(v):
    rows, cols = v.shape
    if cols % 128:
        v = jnp.concatenate([v, jnp.zeros((rows, 128 - cols % 128), f32)], axis=1)
    if rows % 128:
        v = jnp.concatenate([v, jnp.zeros((128 - rows % 128, v.shape[1]), f32)], axis=0)
    return v.T


def column(row):
    m = row.shape[1]
    same = iota((m, m), 0) == iota((m, m), 1)
    return jnp.sum(jnp.where(same, jnp.broadcast_to(row, (m, m)), 0.0), axis=1, keepdims=True)


def flat_row(x, first, width):
    peers, slots = x.shape
    lane = iota((slots, width), 1)
    hot = (lane % slots == iota((slots, width), 0)).astype(f32)
    wide = pick_dot(x, hot)
    mine = (iota((peers, width), 1) + first) // slots == iota((peers, width), 0)
    return jnp.sum(jnp.where(mine, wide, 0.0), axis=0, keepdims=True)


def keep(ref, k, v):
    ref[k] = jnp.broadcast_to(v[:, None, :], (v.shape[0], 8, v.shape[1]))


def slot_of(dx, dy):
    return (dx + 1) * 3 + dy + 1


def kernel(
    n_gx, n_gy,
    *refs,
):
    inputs, outputs = refs[:N_IN], refs[N_IN : N_IN + 2]
    held, rest = refs[N_IN + 2 : 2 * N_IN + 2], refs[2 * N_IN + 2 :]
    copies = [
        pltpu.make_async_copy(src, dst, rest[-1].at[k])
        for k, (src, dst) in enumerate(zip(inputs, held))
    ]
    for copy in copies:
        copy.start()
    work(n_gx, n_gy, copies, *held, *outputs, *rest[:-1])


def work(
    n_gx, n_gy, copies,
    diff_ref, base_ref, couple_ref, rows_ref, cols_ref, dirs_ref,
    cell_ref, weight_ref, count_ref, gauge_ref, prec_ref,
    read_ref, hess_ref,
    pc, pt, pb, rc, rr, coef, gcoef, first_sc, pert, ta, ha, tb, hb, pk, qb, rb, vr, load, grad,
    proj, rsb, agb,
    near_send, near_recv, own_send, own_recv, back_send, back_recv,
    rs_send, rs_recv, ag_send, ag_recv,
):
    gx, gy = lax.axis_index("gx"), lax.axis_index("gy")
    n = n_gx * n_gy
    me = gx * n_gy + gy
    height, breadth = diff_ref.shape
    n_dirs, modes_y, modes_x = dirs_ref.shape
    peers, slots = cell_ref.shape[2], cell_ref.shape[3]
    gauges = prec_ref.shape[2]
    entries = peers * slots
    width = min(entries, 128)
    chunks = entries // width
    ext = height + 2 * PAD
    half = breadth // 2
    meta_c, meta_r = 3 * height + modes_y, 4 * PAD

    rc[...] = jnp.zeros_like(rc)
    rr[...] = jnp.zeros_like(rr)
    vr[...] = jnp.zeros_like(vr)

    barrier = pltpu.get_barrier_semaphore()

    def greet(i, carry):
        t = lax.rem(me + i, n)
        pl.semaphore_signal(
            barrier, inc=1, device_id=(t // n_gy, lax.rem(t, n_gy)),
            device_id_type=pl.DeviceIdType.MESH,
        )
        return carry

    lax.fori_loop(1, n, greet, 0)

    for copy in copies:
        copy.wait()

    live = iota((peers, slots), 1).astype(f32) < column(count_ref[0].astype(f32))
    factor = jnp.where(live, weight_ref[0, 0], 0.0)
    cells = cell_ref[0, 0]
    cell_x, cell_y = (cells // breadth).astype(f32), (cells % breadth).astype(f32)
    pt[...] = jnp.zeros_like(pt)
    pb[...] = jnp.zeros_like(pb)
    pc[meta_c : meta_c + 8, :] = jnp.zeros((8, breadth), f32)
    my_rows = []
    for c in range(chunks):
        trio = [flat_row(v, c * width, width) for v in (cell_x, cell_y, factor)]
        my_rows.append(trio)
        for k, row in enumerate(trio):
            at = 2 * k + c
            pc[meta_c + at : meta_c + at + 1, :width] = row
            pt[meta_r + at : meta_r + at + 1, :width] = row
            pb[meta_r + at : meta_r + at + 1, :width] = row
    for k, ref in enumerate((diff_ref, base_ref, couple_ref)):
        pc[k * height : (k + 1) * height, :] = ref[...]
        pt[k * PAD : (k + 1) * PAD, :] = ref[:PAD, :]
        pb[k * PAD : (k + 1) * PAD, :] = ref[height - PAD :, :]
    pt[3 * PAD : 4 * PAD, :modes_x] = rows_ref[:PAD, :]
    pb[3 * PAD : 4 * PAD, :modes_x] = rows_ref[height - PAD :, :]
    cols_t = cols_ref[...]
    pc[3 * height : 3 * height + modes_y, :] = cols_t

    pl.semaphore_wait(barrier, n - 1)

    def exists(dx, dy):
        ok = None
        for d, at, size in ((dx, gx, n_gx), (dy, gy, n_gy)):
            if d:
                here = at > 0 if d < 0 else at < size - 1
                ok = here if ok is None else jnp.logical_and(ok, here)
        return ok

    def near_ref(dx, dy):
        if dx == 0:
            return rc.at[(dy + 1) // 2]
        return rr.at[(dx + 1) // 2 * 3 + dy + 1]

    def near_copy(dx, dy):
        src = pc if dx == 0 else (pt if dx < 0 else pb)
        return pltpu.make_async_remote_copy(
            src_ref=src, dst_ref=near_ref(-dx, -dy),
            send_sem=near_send.at[slot_of(dx, dy)], recv_sem=near_recv.at[slot_of(-dx, -dy)],
            device_id=(gx + dx, gy + dy), device_id_type=pl.DeviceIdType.MESH,
        )

    sides = [(dx, dy) for dx in (0, -1, 1) for dy in (-1, 0, 1) if dx or dy]
    for dx, dy in sides:

        @pl.when(exists(dx, dy))
        def _(dx=dx, dy=dy):
            near_copy(dx, dy).start()

    for dx, dy in sides:

        @pl.when(exists(dx, dy))
        def _(dx=dx, dy=dy):
            near_copy(-dx, -dy).wait_recv()

    def joined(middle, right, left):
        return jnp.concatenate([middle, jnp.where(iota(right.shape, 1) < half, right, left)], axis=1)

    def extended(k, ref):
        tile = slice(k * PAD, (k + 1) * PAD)
        block = slice(k * height, (k + 1) * height)
        stack = lambda dy, mid: jnp.concatenate(
            [rr[dy + 1, tile, :], mid, rr[3 + dy + 1, tile, :]], axis=0
        )
        return joined(stack(0, ref[...]), stack(1, rc[1, block, :]), stack(-1, rc[0, block, :]))

    diff = extended(0, diff_ref)
    base = extended(1, base_ref)
    couple = extended(2, couple_ref)
    row_at, lane_at = iota((ext, 2 * breadth), 0), iota((ext, 2 * breadth), 1)
    out_row = jnp.logical_or(
        jnp.logical_and(row_at < PAD, gx == 0),
        jnp.logical_and(row_at >= PAD + height, gx == n_gx - 1),
    )
    out_col = jnp.logical_or(
        jnp.logical_and(
            jnp.logical_and(lane_at >= breadth, lane_at < breadth + half), gy == n_gy - 1
        ),
        jnp.logical_and(lane_at >= breadth + half, gy == 0),
    )
    inside = jnp.where(jnp.logical_or(out_row, out_col), 0.0, 1.0).astype(f32)
    centre = inside
    s_sum = jnp.zeros_like(diff)
    own = (slice(PAD, PAD + height), slice(0, breadth))
    for k, (d_near, b_near) in enumerate(zip(around(diff), around(base))):
        weight = (step_ratio * 0.5) * (diff + d_near) * inside
        keep(coef, 1 + k, weight)
        centre = centre - weight
        gap = 0.5 * (b_near - base)
        keep(gcoef, k, (diff * gap)[own])
        pull = step_ratio * gap * inside
        keep(coef, 9 + k, pull)
        s_sum = s_sum + pull
    keep(coef, 0, centre)
    keep(coef, 5, step_ratio * inside)
    keep(coef, 6, couple)
    keep(coef, 7, diff)
    keep(coef, 8, s_sum)

    rows_ext = jnp.concatenate(
        [rr[1, 3 * PAD : 4 * PAD, :modes_x], rows_ref[...], rr[4, 3 * PAD : 4 * PAD, :modes_x]],
        axis=0,
    )
    own_cols = slice(3 * height, 3 * height + modes_y)
    cols_ext = joined(cols_t, rc[1, own_cols, :], rc[0, own_cols, :])
    group = 128 // modes_y
    quads = n_dirs // group
    lane_group = iota((ext, 128), 1) // modes_y
    for q in range(quads):
        block = dirs_ref[q * group : (q + 1) * group].reshape(128, modes_x)
        both = dot(rows_ext, block, NT)
        for j in range(group):
            rows = pl.ds(q * group + j, ext, stride=n_dirs)
            first_sc[rows, :] = jnp.where(lane_group == j, both, 0.0)
    stacked = jnp.concatenate([cols_ext] * group, axis=0)
    wide = (ext, n_dirs, 2 * breadth)

    def perturb(i, carry):
        rows = pl.ds(pl.multiple_of(i * 8 * n_dirs, 8 * n_dirs), 8 * n_dirs)
        p = dot(first_sc[rows, :], stacked).reshape((8,) + wide[1:])
        c = coef[7, pl.ds(i * 8, 8)]
        for g in range(0, n_dirs, 8):
            load[pl.ds(i * 8, 8), g : g + 8, :] = c * p[:, g : g + 8]
        return carry

    lax.fori_loop(0, ext // 8, perturb, 0)

    def sides_of(v):
        size = v.shape[-1]
        return pltpu.roll(v, 1, 2), pltpu.roll(v, size - 1, 2)

    def near_of(ref, x, middle):
        return (ref[pl.ds(x - 1, BLOCK)], ref[pl.ds(x + 1, BLOCK)]) + sides_of(middle)

    def times(k, x, v):
        c = coef[k, pl.ds(x, BLOCK)]
        return jnp.concatenate(
            [c * v[:, g * 8 : (g + 1) * 8] for g in range(n_dirs // 8)], axis=1
        )

    def over_rows(margin, body):
        blocks = (height + 2 * margin) // BLOCK
        unroll = next((u for u in (8, 7, 6, 5) if blocks % u == 0), 0)
        if not unroll:
            blocks += 1
            unroll = next(u for u in (6, 5, 8, 7) if blocks % u == 0)

        def several(i, carry):
            for u in range(unroll):
                body(PAD - margin + (i * unroll + u) * BLOCK)
            return carry

        lax.fori_loop(0, blocks // unroll, several, 0)

    def mixed_with(x, h, ref):
        total = times(0, x, h)
        for k, near in enumerate(near_of(ref, x, h)):
            total = total + times(1 + k, x, near)
        return total

    def stencil(x, t_old, h_old, sign):
        t, h = t_old[pl.ds(x, BLOCK)], h_old[pl.ds(x, BLOCK)]
        total = t
        for near in near_of(t_old, x, t):
            total = total + near
        mixed = mixed_with(x, h, h_old)
        if sign > 0:
            return times(5, x, total) + times(6, x, h), mixed - times(6, x, t)
        return times(5, x, total) - times(6, x, h), mixed + times(6, x, t)

    def make_source(x):
        rows = pl.ds(x, BLOCK)
        p = load[rows]
        total = times(8, x, p)
        for k, near in enumerate(near_of(load, x, p)):
            total = total + times(9 + k, x, near)
        pert[rows] = total

    over_rows(STEPS - 1, make_source)

    pairs = ((ta, ha), (tb, hb))

    def first_step(x):
        rows = pl.ds(x, BLOCK)
        source = pert[rows]
        ta[rows] = times(6, x, source)
        ha[rows] = mixed_with(x, source, pert) + source

    over_rows(STEPS - 2, first_step)
    for i in range(STEPS - 2):
        (t_old, h_old), (t_new, h_new) = pairs[i % 2], pairs[(i + 1) % 2]

        def next_step(x, t_old=t_old, h_old=h_old, t_new=t_new, h_new=h_new):
            rows = pl.ds(x, BLOCK)
            t, h = stencil(x, t_old, h_old, 1)
            t_new[rows] = t
            h_new[rows] = h + pert[rows]

        over_rows(STEPS - 3 - i, next_step)
    hum = pairs[(STEPS - 2) % 2][1]

    humid = hum[PAD : PAD + height, :, :breadth].reshape(height * n_dirs, breadth)
    for c in range(chunks):
        x_row, y_row, f_row = my_rows[c]
        hot = (iota((breadth, width), 0).astype(f32) == y_row).astype(f32)
        picked = pick_dot(humid, hot).reshape(height, n_dirs, width)
        at_x = iota(picked.shape, 0).astype(f32) == x_row[None]
        picked = jnp.sum(jnp.where(at_x, picked, 0.0), axis=0) * f_row
        some = width // slots
        pk[c * some : (c + 1) * some] = turned(picked)[:width].reshape(some, slots, 128)

    def to_owner(o, slot):
        return pltpu.make_async_remote_copy(
            src_ref=pk.at[o], dst_ref=qb.at[slot], send_sem=own_send, recv_sem=own_recv,
            device_id=(o, gy), device_id_type=pl.DeviceIdType.MESH,
        )

    def send_picks(i, carry):
        to_owner(lax.rem(gx + i, n_gx), gx).start()
        return carry

    lax.fori_loop(1, n_gx, send_picks, 0)
    qb[gx] = pk[gx]
    gauge_f = gauge_ref[0, 0].astype(f32)
    hots = []
    for c in range(chunks):
        g_row = flat_row(gauge_f, c * width, width)
        hots.append((iota((128, width), 0).astype(f32) == g_row).astype(f32))
    prec = column(prec_ref[0])
    prec = jnp.concatenate([prec, jnp.zeros((128 - gauges, 1), f32)], axis=0)
    others = pl.ds(0, n_gx - 1)
    everyone = pltpu.make_async_remote_copy(
        src_ref=pk.at[others], dst_ref=qb.at[others], send_sem=own_send, recv_sem=own_recv,
        device_id=(gx, gy), device_id_type=pl.DeviceIdType.MESH,
    )
    everyone.wait_recv()
    some = width // slots
    gauge_read = jnp.zeros((128, 128), f32)
    for c in range(chunks):
        got = qb[c * some : (c + 1) * some].reshape(width, 128)
        gauge_read = gauge_read + dot(hots[c], got)
    weighted = gauge_read * prec
    rb[0] = jnp.zeros((slots, 128), f32)
    rb[n_gx + 1] = jnp.zeros((slots, 128), f32)
    for c in range(chunks):
        back = dot(turned(hots[c])[:width], weighted)
        rb[1 + c * some : 1 + (c + 1) * some] = back.reshape(some, slots, 128)

    def back_copy(t, dy):
        return pltpu.make_async_remote_copy(
            src_ref=rb.at[pl.ds(t, 3)], dst_ref=vr.at[1 - dy, :, gx],
            send_sem=back_send.at[1 + dy], recv_sem=back_recv.at[1 - dy],
            device_id=(t, gy + dy), device_id_type=pl.DeviceIdType.MESH,
        )

    def send_back(i, carry):
        t = lax.rem(gx + i, n_gx)
        for dy in (-1, 1):

            @pl.when(exists(0, dy))
            def _(dy=dy):
                back_copy(t, dy).start()

        @pl.when(i > 0)
        def _():
            back_copy(t, 0).start()

        return carry

    lax.fori_loop(0, n_gx, send_back, 0)
    vr[1, :, gx] = rb[pl.ds(gx, 3)]
    read_ref[0, 0] = gauge_read.T[:n_dirs, :gauges]

    def back_all(dy):
        span = pl.ds(0, n_gx if dy else n_gx - 1)
        return pltpu.make_async_remote_copy(
            src_ref=vr.at[1 + dy, :, span], dst_ref=vr.at[1 + dy, :, span],
            send_sem=back_send.at[1 + dy], recv_sem=back_recv.at[1 + dy],
            device_id=(gx, gy), device_id_type=pl.DeviceIdType.MESH,
        )

    back_all(0).wait_recv()
    for dy in (-1, 1):

        @pl.when(exists(0, dy))
        def _(dy=dy):
            back_all(dy).wait_recv()

    def meta_row(dx, dy, k, c):
        if dx == 0 and dy == 0:
            return my_rows[c][k]
        at = 2 * k + c
        if dx == 0:
            return rc[(dy + 1) // 2, meta_c + at : meta_c + at + 1, :width]
        return rr[(dx + 1) // 2 * 3 + dy + 1, meta_r + at : meta_r + at + 1, :width]

    for dx, at, first, tall in ((-1, 0, height - PAD, PAD), (0, PAD, 0, height), (1, PAD + height, 0, PAD)):
        parts = [None, None]
        for dy in (-1, 0, 1):
            for c in range(chunks):
                x_row, y_row, f_row = (meta_row(dx, dy, k, c) for k in range(3))
                got = vr[dy + 1, dx + 1, c * some : (c + 1) * some].reshape(width, 128)
                values = turned(got)[:n_dirs, :width] * f_row
                at_x = (iota((tall, n_dirs, width), 0) + first).astype(f32) == x_row[None]
                y_at = iota((breadth, width), 0)
                hit_y = y_at.astype(f32) == y_row
                if dy:
                    hit_y = jnp.logical_and(hit_y, y_at < half if dy > 0 else y_at >= half)
                spread_x = jnp.where(at_x, values[None], 0.0)
                term = pick_dot(
                    spread_x.reshape(tall * n_dirs, width), hit_y.astype(f32), NT
                )
                tile = 1 if dy else 0
                parts[tile] = term if parts[tile] is None else parts[tile] + term
        for tile in (0, 1):
            load[at : at + tall, :, tile * breadth : (tile + 1) * breadth] = parts[tile].reshape(
                tall, n_dirs, breadth
            )

    def first_back(x):
        rows = pl.ds(x, BLOCK)
        b = load[rows]
        ta[rows] = -times(6, x, b)
        b_new = mixed_with(x, b, load)
        ha[rows] = b_new
        pert[rows] = b + b_new

    over_rows(STEPS - 1, first_back)
    for i in range(STEPS - 2):
        (t_old, h_old), (t_new, h_new) = pairs[i % 2], pairs[(i + 1) % 2]

        def next_back(x, t_old=t_old, h_old=h_old, t_new=t_new, h_new=h_new):
            rows = pl.ds(x, BLOCK)
            t, h = stencil(x, t_old, h_old, -1)
            t_new[rows] = t
            h_new[rows] = h
            pert[rows] = pert[rows] + h

        over_rows(STEPS - 2 - i, next_back)

    def gradient(x):
        lam = pert[pl.ds(x, BLOCK)]
        total = None
        for k, near in enumerate(near_of(pert, x, lam)):
            gap = step_ratio * (lam - near)[:, :, :breadth]
            c = gcoef[k, pl.ds(x - PAD, BLOCK)]
            term = jnp.concatenate(
                [c * gap[:, g * 8 : (g + 1) * 8] for g in range(n_dirs // 8)], axis=1
            )
            total = term if total is None else total + term
        start = (x - PAD) * n_dirs
        grad[pl.ds(pl.multiple_of(start, 8), BLOCK * n_dirs), :] = total.reshape(
            BLOCK * n_dirs, breadth
        )

    over_rows(0, gradient)

    half_way = None
    for j in range(group):
        pieces = []
        if j:
            pieces.append(jnp.zeros((j * modes_y, breadth), f32))
        pieces.append(cols_t)
        if j < group - 1:
            pieces.append(jnp.zeros(((group - 1 - j) * modes_y, breadth), f32))
        placed = jnp.concatenate(pieces, axis=0)
        mine = jnp.concatenate(
            [grad[pl.ds(q * group + j, height, stride=n_dirs), :] for q in range(quads)], axis=0
        )
        term = dot(mine, placed, NT)
        half_way = term if half_way is None else half_way + term
    rows_t = turned(rows_ref[...])[:modes_x, :height]
    size = proj.shape[1]
    per = modes_x // size
    for q in range(quads):
        both = dot(rows_t, half_way[q * height : (q + 1) * height])
        if per:
            proj[q * per : (q + 1) * per] = both.reshape(per, size, 128)
        else:
            ratio = size // modes_x
            proj[q // ratio, (q % ratio) * modes_x : (q % ratio + 1) * modes_x] = both

    owners = proj.shape[0]

    def share(t):
        return pltpu.make_async_remote_copy(
            src_ref=proj.at[t], dst_ref=rsb.at[me], send_sem=rs_send, recv_sem=rs_recv,
            device_id=(t // n_gy, lax.rem(t, n_gy)), device_id_type=pl.DeviceIdType.MESH,
        )

    def result(t):
        return pltpu.make_async_remote_copy(
            src_ref=agb.at[me], dst_ref=agb.at[me], send_sem=ag_send, recv_sem=ag_recv,
            device_id=(t // n_gy, lax.rem(t, n_gy)), device_id_type=pl.DeviceIdType.MESH,
        )

    def waiter(ref, count, send, recv):
        span = ref.at[pl.ds(0, count)]
        return pltpu.make_async_remote_copy(
            src_ref=span, dst_ref=span, send_sem=send, recv_sem=recv,
            device_id=(gx, gy), device_id_type=pl.DeviceIdType.MESH,
        )

    def send_share(i, carry):
        t = lax.rem(me + i, n)
        if owners == n:
            share(t).start()
        else:

            @pl.when(t < owners)
            def _():
                share(t).start()

        return carry

    lax.fori_loop(1, n, send_share, 0)

    def own_part():
        rsb[me] = proj[me]
        waiter(rsb, n - 1, rs_send, rs_recv).wait_recv()
        agb[me] = jnp.sum(rsb[...], axis=0)

        def send_result(i, carry):
            result(lax.rem(me + i, n)).start()
            return carry

        lax.fori_loop(1, n, send_result, 0)
        if owners > 1:
            waiter(agb, owners - 1, ag_send, ag_recv).wait_recv()
        waiter(rsb, n - 1, ag_send, ag_recv).wait_send()
        if owners > 1:
            waiter(agb, owners - 1, rs_send, rs_recv).wait_send()

    def other_part():
        waiter(agb, owners, ag_send, ag_recv).wait_recv()
        waiter(agb, owners, rs_send, rs_recv).wait_send()

    if owners == n:
        own_part()
    else:
        pl.when(me < owners)(own_part)
        pl.when(me >= owners)(other_part)

    summed = agb[...].reshape(quads, modes_x, 128)
    for q in range(quads):
        dirs = dirs_ref[q * group : (q + 1) * group]
        hess_ref[q * group : (q + 1) * group] = dirs + turned(summed[q])[:, :modes_x].reshape(
            dirs.shape
        )

    for dx, dy in sides:

        @pl.when(exists(dx, dy))
        def _(dx=dx, dy=dy):
            near_copy(dx, dy).wait_send()

    everyone.wait_send()
    back_all(0).wait_send()
    for dy in (-1, 1):

        @pl.when(exists(0, dy))
        def _(dy=dy):
            back_all(dy).wait_send()


def local(n_gx, n_gy, *args):
    args = list(args)
    args[4] = args[4].T
    args[5] = args[5].transpose(0, 2, 1)
    diffusivity, dirs, cells, noise = args[0], args[5], args[6], args[10]
    height, breadth = diffusivity.shape
    n_dirs, modes_y, modes_x = dirs.shape
    peers, slots = cells.shape[2], cells.shape[3]
    gauges = noise.shape[2]
    n = n_gx * n_gy
    ext = height + 2 * PAD
    total_rows = n_dirs * modes_x * modes_y // 128
    size = max(8, total_rows // n)
    owners = total_rows // size
    vmem = lambda *shape: pltpu.VMEM(shape, f32)
    dma = pltpu.SemaphoreType.DMA
    space = pl.BlockSpec(memory_space=pltpu.VMEM)
    readings, hess = pl.pallas_call(
        functools.partial(kernel, n_gx, n_gy),
        out_shape=(
            jax.ShapeDtypeStruct((1, 1, n_dirs, gauges), f32),
            jax.ShapeDtypeStruct(dirs.shape, f32),
        ),
        in_specs=[pl.BlockSpec(memory_space=pltpu.HBM)] * len(args),
        out_specs=(space, space),
        scratch_shapes=[pltpu.VMEM(a.shape, a.dtype) for a in args]
        + [
            vmem(3 * height + modes_y + 8, breadth),
            vmem(5 * PAD, breadth),
            vmem(5 * PAD, breadth),
            vmem(2, 3 * height + modes_y + 8, breadth),
            vmem(6, 5 * PAD, breadth),
            vmem(13, ext, 8, 2 * breadth),
            vmem(4, height, 8, breadth),
            vmem(ext * n_dirs, 128),
            vmem(ext, n_dirs, 2 * breadth),
            vmem(ext, n_dirs, 2 * breadth),
            vmem(ext, n_dirs, 2 * breadth),
            vmem(ext, n_dirs, 2 * breadth),
            vmem(ext, n_dirs, 2 * breadth),
            vmem(peers, slots, 128),
            vmem(peers, slots, 128),
            vmem(peers + 2, slots, 128),
            vmem(3, 3, peers, slots, 128),
            vmem(ext, n_dirs, 2 * breadth),
            vmem(height * n_dirs, breadth),
            vmem(owners, size, 128),
            vmem(n, size, 128),
            vmem(owners, size, 128),
            dma((9,)),
            dma((9,)),
            dma,
            dma,
            dma((3,)),
            dma((3,)),
            dma,
            dma,
            dma,
            dma,
            dma((N_IN,)),
        ],
        compiler_params=pltpu.CompilerParams(
            collective_id=0, has_side_effects=True, vmem_limit_bytes=40 * 1024 * 1024
        ),
    )(*args)
    return readings, hess.transpose(0, 2, 1)


def solution(mesh):
    placed = (
        P("gx", "gy"),
        P("gx", "gy"),
        P("gx", "gy"),
        P("gx", None),
        P("gy", None),
        P(),
        P("gx", "gy", None, None),
        P("gx", "gy", None, None),
        P("gx", "gy", None),
        P("gx", "gy", None, None),
        P("gx", "gy", None),
    )
    return jax.shard_map(
        functools.partial(local, mesh.shape["gx"], mesh.shape["gy"]),
        mesh=mesh,
        in_specs=placed,
        out_specs=(P("gx", "gy", None, None), P()),
        check_vma=False,
    )
```
